32 devices in a mesh: pix: 8 (over z, y), shell: 4 (over x, core).
Axes of the slice: x: 2, y: 2, z: 4, core: 2. Of those that a mesh axis runs over, the one named last changes fastest.
Arguments:
- field: float32 [128, 262144], P('shell', 'pix'), may hold values from -3 to 3
- momentum: float32 [128, 262144], P('shell', 'pix'), may hold values from -6 to 6
- kernels: float32 [4, 20, 128], P(None, None, 'shell'), may hold values from 0.002 to 0.02
- depth_class: int32 [262144], P('pix'), may hold values from 0 to 3
- counts: int32 [20, 262144], P(None, 'pix'), may hold values from 0 to 12
- mask: float32 [262144], P('pix'), may hold values from 0.1 to 1.5, as said below
- mean_counts: float32 [20], replicated, may hold values from 1 to 8
- shell_scale: float32 [128], P('shell'), may hold values from 0.5 to 2
Outputs:
- gradient: float32 [128, 262144], P('shell', 'pix')
- loglik: float32 [], replicated
The draws below stay inside these ranges and needn't reach their ends.
Inputs may be any that keep to these rules, and one draw needn't show every extreme that they name: `mask`: mask weights are positive.
All inputs are finite; a program needn't handle non-finite values.
Results may differ from the reference program's by a relative error of at most 0.00005.
Values sent between devices are 32-bit elements; how exact they have to be, the bound alone decides.
A program may use at most 128 MiB of HBM per device.

```python
import math
import jax
import jax.numpy as jnp
from jax import lax

SHELLS = 128
BINS = 20
CLASSES = 4
CYCLE = 2048
PIX = 262144


def draw_mask(key, part):
    position = jnp.arange(PIX, dtype=jnp.float32) / PIX
    base = 0.5 + position
    factor = jax.random.uniform(key, (PIX,), jnp.float32, 0.4, 1.0)
    return base * factor


def with_ends(result, own_key, low, largest):
    place = [jax.random.randint(jax.random.fold_in(own_key, axis), (), 0, length) for axis, length in enumerate(result.shape)]
    main_axis = result.shape.index(max(result.shape))
    neighbour = place[:main_axis] + [(place[main_axis] + 1) % result.shape[main_axis]] + place[main_axis + 1:]
    return result.at[tuple(place)].set(low).at[tuple(neighbour)].set(largest)


def shard_levels(own_key, extent, pieces, smallest, top_value):
    loudness, own = 1.0, jax.random.fold_in(own_key, 6)
    for axis_at, blocks in pieces:
        steps = jnp.exp(jax.random.uniform(jax.random.fold_in(own, axis_at), (blocks,), jnp.float32, smallest / len(pieces), top_value / len(pieces)))
        loudness = loudness * jnp.repeat(steps, extent[axis_at] // blocks).reshape([-1 if axis == axis_at else 1 for axis in range(len(extent))])
    return loudness


def bell_draw(own_key, extent, width, most, pieces=(), held_as=jnp.bfloat16):
    level = shard_levels(own_key, extent, pieces, -0.22, 0.18) if pieces else 1.0
    array = jax.random.normal(own_key, extent, jnp.float32) * width * level
    return jnp.minimum(jnp.maximum(array, -most), most).astype(held_as)


def setup_inputs(seed: int = 0) -> dict:
    arg_keys = jax.random.split(jax.random.key(seed), 9)
    field = bell_draw(arg_keys[0], (SHELLS, PIX), 0.5, 3.0, ((0, 4), (1, 8)), jnp.float32)
    momentum = bell_draw(arg_keys[1], (SHELLS, PIX), 1.0, 6.0, ((0, 4), (1, 8)), jnp.float32)
    kernels = jnp.clip(jnp.exp(math.log(0.02) - 2.30258502 * jax.random.uniform(arg_keys[2], (CLASSES, BINS, SHELLS), jnp.float32) ** shard_levels(arg_keys[2], (CLASSES, BINS, SHELLS), ((2, 4),), -0.2, 0.2)), 0.002, 0.02)
    depth_class = with_ends(jax.random.randint(arg_keys[3], (PIX,), 0, CLASSES), jax.random.fold_in(arg_keys[3], 1), 0, CLASSES - 1).astype(jnp.int32)
    counts = with_ends(jax.random.randint(arg_keys[4], (BINS, PIX), 0, 13), jax.random.fold_in(arg_keys[4], 1), 0, 12).astype(jnp.int32)
    mask = draw_mask(jax.random.fold_in(arg_keys[8], 71), 0)
    mean_counts = jnp.clip(jnp.exp(jax.random.uniform(arg_keys[6], (BINS,), jnp.float32, math.log(1.0), math.log(8.0))), 1.0, 8.0)
    shell_scale = jnp.clip(jnp.exp(math.log(2.0) - 1.3862944 * jax.random.uniform(arg_keys[7], (SHELLS,), jnp.float32) ** shard_levels(arg_keys[7], (SHELLS,), ((0, 4),), -0.2, 0.2)), 0.5, 2.0)
    return {"field": field, "momentum": momentum, "kernels": kernels, "depth_class": depth_class, "counts": counts, "mask": mask, "mean_counts": mean_counts, "shell_scale": shell_scale}


LEAP = 0.1
ANGULAR = 0.5
RADIAL = 0.5


def reference(field, momentum, kernels, depth_class, counts, mask, mean_counts, shell_scale):
    position = field + LEAP * momentum
    density = jnp.exp(position)
    flat = kernels.reshape(CLASSES * BINS, SHELLS)
    onehot = (depth_class[None, :] == jnp.arange(CLASSES, dtype=jnp.int32)[:, None]).astype(jnp.float32)
    every = jnp.dot(flat, density, precision=lax.Precision.HIGHEST, preferred_element_type=jnp.float32)
    proj = jnp.sum(every.reshape(CLASSES, BINS, PIX) * onehot[:, None, :], axis=0)
    weighted = jnp.sum(mask[None, :] * proj, axis=1)
    norm = weighted / PIX
    counted = counts.astype(jnp.float32)
    total = jnp.sum(counted, axis=1)
    rate = mean_counts[:, None] * mask[None, :] * proj / norm[:, None]
    loglik = jnp.sum(counted * jnp.log(rate) - rate) / (BINS * PIX)
    ratio = counted / proj - (total / (PIX * norm))[:, None] * mask[None, :]
    spread = (onehot[:, None, :] * ratio[None, :, :]).reshape(CLASSES * BINS, PIX)
    back = jnp.dot(flat.T, spread, precision=lax.Precision.HIGHEST, preferred_element_type=jnp.float32)
    like = density * back
    padded = jnp.pad(position, ((0, 0), (CYCLE, CYCLE)))
    angular = 4.0 * position - padded[:, CYCLE - 1:CYCLE - 1 + PIX] - padded[:, CYCLE + 1:CYCLE + 1 + PIX]
    angular = angular - padded[:, 0:PIX] - padded[:, 2 * CYCLE:2 * CYCLE + PIX]
    stacked = jnp.pad(position, ((1, 1), (0, 0)))
    radial = 2.0 * position - stacked[:-2] - stacked[2:]
    gradient = like - position / (shell_scale[:, None] * shell_scale[:, None]) - ANGULAR * angular - RADIAL * radial
    return gradient, loglik
```

```python
import functools

import jax
import jax.numpy as jnp
from jax import lax
from jax.experimental import pallas as pl
from jax.experimental.pallas import tpu as pltpu
from jax.sharding import PartitionSpec as P

CYCLE = 2048

LEAP = 0.1
ANGULAR = 0.5
RADIAL = 0.5
MESH = pl.DeviceIdType.MESH
F32 = jnp.float32
BF16 = jnp.bfloat16
LANES = 128


def halves(value):
    high = value.astype(BF16)
    return high, (value - high.astype(F32)).astype(BF16)


def kernel(
    sizes,
    field, momentum, weight, weight_t, classes_of, counts, mask, mean, diag,
    out, loglik,
    pos, dens, part_send, part_own, part_recv, group_send, group_recv, ratio,
    low_send, high_send, low_recv, high_recv, acc, red_send, red_recv, log_send, log_recv,
    w_front, w_back,
    a_sems, b_send_sems, b_recv_sems, c_sems, halo_sems, edge_sems, red_sems, log_sems,
):
    pix_count, shell_count, classes, bins, chunk, chunks = sizes
    chips = shell_count // 2
    shells, pixels = field.shape
    padded = weight.shape[0] // classes
    half = chunk // 2
    total_pix = pixels * pix_count
    p, s = lax.axis_index("pix"), lax.axis_index("shell")
    core, chip = s % 2, s // 2

    def flip(index, step):
        return index + step - 2 * step * ((index // step) % 2)

    mate = (p, flip(s, 1))
    peers = [(p, ((chip + d) % chips) * 2 + core) for d in range(1, chips)]
    rounds = []
    step = 1
    while step < shell_count:
        rounds.append((p, flip(s, step)))
        step *= 2
    step = 1
    while step < pix_count:
        rounds.append((flip(p, step), s))
        step *= 2
    right, left = (p + 1) % pix_count, (p + pix_count - 1) % pix_count
    above, below = (s + 1) % shell_count, (s + shell_count - 1) % shell_count
    greeted = rounds + peers + [(right, s), (left, s), (p, above), (p, below)]
    barrier = pltpu.get_barrier_semaphore()
    for device in greeted:
        pl.semaphore_signal(barrier, inc=1, device_id=device, device_id_type=MESH)

    w_high, w_low = halves(weight[...])
    w_front[...] = jnp.concatenate([w_high, w_high, w_low], axis=1)
    t_high, t_low = halves(weight_t[...])
    w_back[...] = jnp.concatenate(
        [
            jnp.concatenate([t_high, t_high], axis=1),
            jnp.concatenate([t_low, jnp.zeros_like(t_low)], axis=1),
        ],
        axis=0,
    )
    acc[...] = jnp.zeros_like(acc)

    def copy_to(device, src, dst, send_sem, recv_sem):
        return pltpu.make_async_remote_copy(
            src_ref=src, dst_ref=dst, send_sem=send_sem, recv_sem=recv_sem,
            device_id=device, device_id_type=MESH,
        )

    def columns(j, lead=0):
        return pl.ds(pl.multiple_of(j * chunk + lead, LANES), chunk)

    def front(j, target):
        cols = columns(j)
        here = field[:, cols] + LEAP * momentum[:, cols]
        pos[:, columns(j, CYCLE)] = here
        low_send[:, cols] = here[0:1]
        high_send[:, cols] = here[shells - 1 : shells]
        density = jnp.exp(here)
        dens[:, cols] = density
        high, low = halves(density)
        every = jnp.dot(
            w_front[...], jnp.concatenate([high, low, high], axis=0), preferred_element_type=F32
        )
        kind = jnp.broadcast_to(classes_of[:, cols], (padded, chunk))
        part = every[:padded]
        for c in range(1, classes):
            part = jnp.where(kind == c, every[c * padded : (c + 1) * padded], part)
        target[...] = part
        acc[0] += mask[:, cols] * part
        acc[1, 0:bins] += counts[:, cols].astype(F32)

    def a_copy(k):
        return copy_to(mate, part_send.at[k], part_recv.at[k], a_sems.at[0, k], a_sems.at[1, k])

    def b_copy(k, d):
        return copy_to(
            peers[d], group_send.at[k], group_recv.at[d, k], b_send_sems.at[d, k], b_recv_sems.at[d, k]
        )

    def forward(k):
        a_copy(k).wait_recv()
        both = part_own[k] + part_recv[k]
        full = bins // 8
        for i in range(2):
            for r in range(full):
                group_send[k, i * full + r] = both[r * 8 : r * 8 + 8, i * half : (i + 1) * half]
        group_send[k, 2 * full] = jnp.concatenate(
            [both[full * 8 : bins, :half], both[full * 8 : bins, half:]], axis=0
        )
        for d in range(chips - 1):
            b_copy(k, d).start()

    other = 1 - core
    front(other * chunks, part_send.at[0])
    pl.semaphore_wait(barrier, len(greeted))
    a_copy(0).start()
    front(core * chunks, part_own.at[0])

    def front_step(k, carry):
        front(other * chunks + k, part_send.at[k])
        front(core * chunks + k, part_own.at[k])
        a_copy(k).start()
        forward(k - 1)
        return carry

    lax.fori_loop(1, chunks, front_step, 0)
    forward(chunks - 1)

    to_right = copy_to(
        (right, s), pos.at[:, pl.ds(pixels, CYCLE)], pos.at[:, pl.ds(0, CYCLE)],
        halo_sems.at[0], halo_sems.at[1],
    )
    to_left = copy_to(
        (left, s), pos.at[:, pl.ds(CYCLE, CYCLE)], pos.at[:, pl.ds(pixels + CYCLE, CYCLE)],
        halo_sems.at[2], halo_sems.at[3],
    )
    to_above = copy_to((p, above), high_send, low_recv, edge_sems.at[0], edge_sems.at[1])
    to_below = copy_to((p, below), low_send, high_recv, edge_sems.at[2], edge_sems.at[3])
    has_right, has_left = p < pix_count - 1, p > 0
    has_above, has_below = s < shell_count - 1, s > 0
    pl.when(has_right)(lambda: to_right.start())
    pl.when(has_left)(lambda: to_left.start())
    pl.when(has_above)(lambda: to_above.start())
    pl.when(has_below)(lambda: to_below.start())

    @pl.when(p == 0)
    def _():
        pos[:, 0:CYCLE] = jnp.zeros((shells, CYCLE), F32)

    @pl.when(p == pix_count - 1)
    def _():
        pos[:, pixels + CYCLE :] = jnp.zeros((shells, CYCLE), F32)

    @pl.when(s == 0)
    def _():
        low_recv[...] = jnp.zeros_like(low_recv)

    @pl.when(s == shell_count - 1)
    def _():
        high_recv[...] = jnp.zeros_like(high_recv)

    lane = lax.broadcasted_iota(jnp.int32, (padded, LANES), 1)
    weighted = jnp.sum(acc[0], axis=1, keepdims=True)
    counted = jnp.sum(acc[1], axis=1, keepdims=True) * (1.0 / shell_count)
    red_send[0] = jnp.where(lane < LANES // 2, weighted, counted)

    def butterfly(sent, received, sems):
        for i, device in enumerate(rounds):
            copy = copy_to(device, sent.at[i], received.at[i], sems.at[0, i], sems.at[1, i])
            copy.start()
            copy.wait()
            sent[i + 1] = sent[i] + received[i]

    butterfly(red_send, red_recv, red_sems)
    sums = red_send[len(rounds)]
    norm = sums[:, 0:1] * (1.0 / total_pix)
    total = sums[:, LANES - 1 : LANES]
    row = lax.broadcasted_iota(jnp.int32, (padded, 1), 0)
    norm = jnp.where(row < bins, norm, 1.0)
    coefficient = (total / (total_pix * norm))[:bins]
    acc[0] = jnp.zeros((padded, chunk), F32)

    pl.when(has_right)(lambda: to_right.wait_send())
    pl.when(has_left)(lambda: to_left.wait_send())
    pl.when(has_above)(lambda: to_above.wait_send())
    pl.when(has_below)(lambda: to_below.wait_send())
    pl.when(has_left)(lambda: to_right.wait_recv())
    pl.when(has_right)(lambda: to_left.wait_recv())
    pl.when(has_below)(lambda: to_above.wait_recv())
    pl.when(has_above)(lambda: to_below.wait_recv())

    scaled = diag[...]

    def stencil_step(j, carry):
        cols = columns(j)
        wide = pos[:, pl.ds(pl.multiple_of(j * chunk + CYCLE - LANES, LANES), chunk + 2 * LANES)]
        here = wide[:, LANES : LANES + chunk]
        around = (
            wide[:, LANES - 1 : LANES - 1 + chunk]
            + wide[:, LANES + 1 : LANES + 1 + chunk]
            + pos[:, columns(j)]
            + pos[:, columns(j, 2 * CYCLE)]
        )
        lower = jnp.concatenate([low_recv[:, cols], here[:-1]], axis=0)
        upper = jnp.concatenate([here[1:], high_recv[:, cols]], axis=0)
        out[:, cols] = ANGULAR * around + RADIAL * (lower + upper) - here * scaled
        return carry

    lax.fori_loop(0, pixels // chunk, stencil_step, 0)

    def c_copy(k):
        block = core * chunks + k
        return copy_to(mate, ratio.at[block], ratio.at[block], c_sems.at[0, k], c_sems.at[1, k])

    def unpacked(ref):
        full = bins // 8
        return jnp.concatenate(
            [
                jnp.concatenate(
                    [ref[i * full + r] for r in range(full)]
                    + [ref[2 * full][i * (bins % 8) : (i + 1) * (bins % 8)]],
                    axis=0,
                )
                for i in range(2)
            ],
            axis=1,
        )

    def back(j):
        cols = columns(j)
        kind = jnp.broadcast_to(classes_of[:, cols], (padded, chunk))
        value = ratio[j]
        high = value.astype(BF16).astype(F32)
        low = value - high
        spread = jnp.concatenate(
            [jnp.where(kind == c, x, 0.0).astype(BF16) for x in (high, low)
             for c in range(classes)],
            axis=0,
        ) if padded % 16 == 0 else jnp.concatenate(
            [jnp.where(kind == c, x, 0.0) for x in (high, low) for c in range(classes)], axis=0
        ).astype(BF16)
        both = jnp.dot(w_back[...], spread, preferred_element_type=F32)
        out[:, cols] += dens[:, cols] * (both[:shells] + both[shells:])

    def ratio_step(k, carry):
        for d in range(chips - 1):
            b_copy(k, d).wait_recv()
        block = core * chunks + k
        cols = columns(block)
        proj = unpacked(group_send.at[k])
        for d in range(chips - 1):
            proj = proj + unpacked(group_recv.at[d, k])
        number = counts[:, cols].astype(F32)
        masked = mask[:, cols]
        ratio[block, 0:bins] = number / proj - coefficient * masked
        ratio[block, bins:padded] = jnp.zeros((padded - bins, chunk), F32)
        acc[0, 0:bins] += number * jnp.log(masked * proj)
        c_copy(k).start()
        back(block)
        return carry

    def partner_step(k):
        c_copy(k).wait_recv()
        back(other * chunks + k)

    ratio_step(0, 0)

    def loop_step(k, carry):
        ratio_step(k, 0)
        partner_step(k - 1)
        return carry

    lax.fori_loop(1, chunks, loop_step, 0)
    own_log = jnp.sum(jnp.sum(acc[0], axis=1, keepdims=True), axis=0, keepdims=True)
    log_send[0] = jnp.broadcast_to(own_log * (1.0 / chips), (8, LANES))
    partner_step(chunks - 1)
    butterfly(log_send, log_recv, log_sems)

    safe_mean = jnp.where(row < bins, mean[...], 1.0)
    per_bin = jnp.where(
        row < bins, total * jnp.log(safe_mean / norm) - safe_mean * total_pix, 0.0
    )
    rest = jnp.sum(jnp.broadcast_to(per_bin, (padded, LANES)), axis=0, keepdims=True)
    loglik[...] = (log_send[len(rounds)] + rest) * (1.0 / (bins * total_pix))

    def drain(k, carry):
        a_copy(k).wait_send()
        for d in range(chips - 1):
            b_copy(k, d).wait_send()
        c_copy(k).wait_send()
        return carry

    lax.fori_loop(0, chunks, drain, 0)


def shards(pix_count, shell_count, field, momentum, kernels, depth_class, counts, mask, mean_counts, shell_scale):
    shells, pixels = field.shape
    classes, bins, _ = kernels.shape
    padded = -(-bins // 8) * 8
    assert bins % 8 == 4
    chunk = 1024
    while pixels % (2 * chunk):
        chunk //= 2
    chunks = pixels // (2 * chunk)
    chips = shell_count // 2
    weight = jnp.pad(kernels, ((0, 0), (0, padded - bins), (0, 0))).reshape(classes * padded, shells)
    mean = jnp.pad(mean_counts, (0, padded - bins), constant_values=1.0)[:, None]
    diag = (1.0 / (shell_scale * shell_scale) + 4.0 * ANGULAR + 2.0 * RADIAL)[:, None]
    steps = (pix_count.bit_length() - 1) + (shell_count.bit_length() - 1)
    tiles = 2 * (bins // 8) + 1
    vmem = pltpu.VMEM
    dma = pltpu.SemaphoreType.DMA
    edge = vmem((1, pixels), F32)
    part = vmem((chunks, padded, chunk), F32)
    scratch = [
        vmem((shells, pixels + 2 * CYCLE), F32),
        vmem((shells, pixels), F32),
        part, part, part,
        vmem((chunks, tiles, 8, chunk // 2), F32),
        vmem((chips - 1, chunks, tiles, 8, chunk // 2), F32),
        vmem((2 * chunks, padded, chunk), F32),
        edge, edge, edge, edge,
        vmem((2, padded, chunk), F32),
        vmem((steps + 1, padded, LANES), F32),
        vmem((steps, padded, LANES), F32),
        vmem((steps + 1, 8, LANES), F32),
        vmem((steps, 8, LANES), F32),
        vmem((classes * padded, 3 * shells), BF16),
        vmem((2 * shells, 2 * classes * padded), BF16),
        dma((2, chunks)),
        dma((chips - 1, chunks)),
        dma((chips - 1, chunks)),
        dma((2, chunks)),
        dma((4,)),
        dma((4,)),
        dma((2, steps)),
        dma((2, steps)),
    ]
    gradient, loglik = pl.pallas_call(
        functools.partial(kernel, (pix_count, shell_count, classes, bins, chunk, chunks)),
        out_shape=(
            jax.ShapeDtypeStruct((shells, pixels), F32),
            jax.ShapeDtypeStruct((8, LANES), F32),
        ),
        in_specs=[pl.BlockSpec(memory_space=pltpu.VMEM)] * 9,
        out_specs=(pl.BlockSpec(memory_space=pltpu.VMEM), pl.BlockSpec(memory_space=pltpu.VMEM)),
        scratch_shapes=scratch,
        compiler_params=pltpu.CompilerParams(
            collective_id=0, has_side_effects=True, vmem_limit_bytes=56 * 2**20
        ),
    )(
        field, momentum, weight, weight.T, depth_class[None, :], counts, mask[None, :], mean, diag
    )
    return gradient, loglik[0, 0]


def solution(mesh):
    placed = (
        P("shell", "pix"),
        P("shell", "pix"),
        P(None, None, "shell"),
        P("pix"),
        P(None, "pix"),
        P("pix"),
        P(),
        P("shell"),
    )
    return jax.shard_map(
        functools.partial(shards, mesh.shape["pix"], mesh.shape["shell"]),
        mesh=mesh,
        in_specs=placed,
        out_specs=(P("shell", "pix"), P()),
        check_vma=False,
    )
```

```python
import functools

import jax
import jax.numpy as jnp
from jax import lax
from jax.experimental import pallas as pl
from jax.experimental.pallas import tpu as pltpu
from jax.sharding import PartitionSpec as P

CYCLE = 2048

LEAP = 0.1
ANGULAR = 0.5
RADIAL = 0.5
MESH = pl.DeviceIdType.MESH
F32 = jnp.float32
BF16 = jnp.bfloat16
LANES = 128


def halves(value):
    high = value.astype(BF16)
    return high, (value - high.astype(F32)).astype(BF16)


def kernel(
    sizes,
    field, momentum, weight, weight_t, classes_of, counts, mask, mean, diag,
    out, loglik,
    pos, dens, part_send, part_own, part_recv, group_send, group_recv, ratio,
    low_send, high_send, low_recv, high_recv, acc, red_send, red_recv, log_send, log_recv, shares,
    w_front, w_back,
    a_sems, b_send_sems, b_recv_sems, c_sems, halo_sems, edge_sems, red_sems, log_sems, share_sems,
):
    pix_count, shell_count, classes, bins, chunk, chunks = sizes
    chips = shell_count // 2
    shells, pixels = field.shape
    padded = weight.shape[0] // classes
    half = chunk // 2
    total_pix = pixels * pix_count
    p, s = lax.axis_index("pix"), lax.axis_index("shell")
    core, chip = s % 2, s // 2

    def flip(index, step):
        return index + step - 2 * step * ((index // step) % 2)

    mate = (p, flip(s, 1))
    peers = [(p, ((chip + d) % chips) * 2 + core) for d in range(1, chips)]
    rounds = []
    step = 1
    while step < shell_count:
        rounds.append((p, flip(s, step)))
        step *= 2
    step = 1
    while step < pix_count:
        rounds.append((flip(p, step), s))
        step *= 2
    log_rounds = [mate]
    if chips > 2:
        log_rounds += rounds[1 : shell_count.bit_length() - 1]
    across = [((p + d) % pix_count, s) for d in range(1, pix_count)]
    right, left = (p + 1) % pix_count, (p + pix_count - 1) % pix_count
    above, below = (s + 1) % shell_count, (s + shell_count - 1) % shell_count
    greeted = rounds[: shell_count.bit_length() - 1] + peers + across + [(p, above), (p, below)]
    barrier = pltpu.get_barrier_semaphore()
    for device in greeted:
        pl.semaphore_signal(barrier, inc=1, device_id=device, device_id_type=MESH)

    w_high, w_low = halves(weight[...])
    w_front[...] = jnp.concatenate([w_high, w_high, w_low], axis=1)
    t_high, t_low = halves(weight_t[...])
    w_back[...] = jnp.concatenate(
        [
            jnp.concatenate([t_high, t_high], axis=1),
            jnp.concatenate([t_low, jnp.zeros_like(t_low)], axis=1),
        ],
        axis=0,
    )
    acc[...] = jnp.zeros_like(acc)

    def copy_to(device, src, dst, send_sem, recv_sem):
        return pltpu.make_async_remote_copy(
            src_ref=src, dst_ref=dst, send_sem=send_sem, recv_sem=recv_sem,
            device_id=device, device_id_type=MESH,
        )

    def columns(j, lead=0):
        return pl.ds(pl.multiple_of(j * chunk + lead, LANES), chunk)

    def front(j, target):
        cols = columns(j)
        here = field[:, cols] + LEAP * momentum[:, cols]
        pos[:, columns(j, CYCLE)] = here
        density = jnp.exp(here)
        dens[:, cols] = density
        high, low = halves(density)
        every = jnp.dot(
            w_front[...], jnp.concatenate([high, low, high], axis=0), preferred_element_type=F32
        )
        kind = jnp.broadcast_to(classes_of[:, cols], (padded, chunk))
        part = every[:padded]
        for c in range(1, classes):
            part = jnp.where(kind == c, every[c * padded : (c + 1) * padded], part)
        target[...] = part
        acc[0] += mask[:, cols] * part
        acc[1, 0:bins] += counts[:, cols].astype(F32)

    def a_copy(k):
        return copy_to(mate, part_send.at[k], part_recv.at[k], a_sems.at[0, k], a_sems.at[1, k])

    def b_copy(k, d):
        return copy_to(
            peers[d], group_send.at[k], group_recv.at[d, k], b_send_sems.at[d, k], b_recv_sems.at[d, k]
        )

    def forward(k):
        a_copy(k).wait_recv()
        both = part_own[k] + part_recv[k]
        full = bins // 8
        for i in range(2):
            for r in range(full):
                group_send[k, i * full + r] = both[r * 8 : r * 8 + 8, i * half : (i + 1) * half]
        group_send[k, 2 * full] = jnp.concatenate(
            [both[full * 8 : bins, :half], both[full * 8 : bins, half:]], axis=0
        )
        for d in range(chips - 1):
            b_copy(k, d).start()

    other = 1 - core
    low_send[...] = field[0:1, :] + LEAP * momentum[0:1, :]
    high_send[...] = field[shells - 1 : shells, :] + LEAP * momentum[shells - 1 : shells, :]
    to_above = copy_to((p, above), high_send, low_recv, edge_sems.at[0], edge_sems.at[1])
    to_below = copy_to((p, below), low_send, high_recv, edge_sems.at[2], edge_sems.at[3])
    has_above, has_below = s < shell_count - 1, s > 0
    front(other * chunks, part_send.at[0])
    pl.semaphore_wait(barrier, len(greeted))
    pl.when(has_above)(lambda: to_above.start())
    pl.when(has_below)(lambda: to_below.start())
    a_copy(0).start()
    front(core * chunks, part_own.at[0])

    def front_step(k, carry):
        front(other * chunks + k, part_send.at[k])
        front(core * chunks + k, part_own.at[k])
        a_copy(k).start()
        forward(k - 1)
        return carry

    lax.fori_loop(1, chunks, front_step, 0)
    forward(chunks - 1)

    to_right = copy_to(
        (right, s), pos.at[:, pl.ds(pixels, CYCLE)], pos.at[:, pl.ds(0, CYCLE)],
        halo_sems.at[0], halo_sems.at[1],
    )
    to_left = copy_to(
        (left, s), pos.at[:, pl.ds(CYCLE, CYCLE)], pos.at[:, pl.ds(pixels + CYCLE, CYCLE)],
        halo_sems.at[2], halo_sems.at[3],
    )
    has_right, has_left = p < pix_count - 1, p > 0
    pl.when(has_right)(lambda: to_right.start())
    pl.when(has_left)(lambda: to_left.start())

    @pl.when(p == 0)
    def _():
        pos[:, 0:CYCLE] = jnp.zeros((shells, CYCLE), F32)

    @pl.when(p == pix_count - 1)
    def _():
        pos[:, pixels + CYCLE :] = jnp.zeros((shells, CYCLE), F32)

    @pl.when(s == 0)
    def _():
        low_recv[...] = jnp.zeros_like(low_recv)

    @pl.when(s == shell_count - 1)
    def _():
        high_recv[...] = jnp.zeros_like(high_recv)

    lane = lax.broadcasted_iota(jnp.int32, (padded, LANES), 1)
    weighted = jnp.sum(acc[0], axis=1, keepdims=True)
    counted = jnp.sum(acc[1], axis=1, keepdims=True) * (1.0 / shell_count)
    red_send[0] = jnp.where(lane < LANES // 2, weighted, counted)

    scaled = diag[...]

    def stencil_step(j, carry):
        cols = columns(j)
        wide = pos[:, pl.ds(pl.multiple_of(j * chunk + CYCLE - LANES, LANES), chunk + 2 * LANES)]
        here = wide[:, LANES : LANES + chunk]
        around = (
            wide[:, LANES - 1 : LANES - 1 + chunk]
            + wide[:, LANES + 1 : LANES + 1 + chunk]
            + pos[:, columns(j)]
            + pos[:, columns(j, 2 * CYCLE)]
        )
        lower = jnp.concatenate([jnp.zeros((1, chunk), F32), here[:-1]], axis=0)
        upper = jnp.concatenate([here[1:], jnp.zeros((1, chunk), F32)], axis=0)
        out[:, cols] = ANGULAR * around + RADIAL * (lower + upper) - here * scaled
        return carry

    blocks, border = pixels // chunk, -(-CYCLE // chunk)
    inner = max(blocks - 2 * border, 0)
    for i, device in enumerate(rounds):
        copy = copy_to(device, red_send.at[i], red_recv.at[i], red_sems.at[0, i], red_sems.at[1, i])
        copy.start()
        lax.fori_loop(
            border + inner * i // len(rounds),
            border + inner * (i + 1) // len(rounds),
            stencil_step,
            0,
        )
        copy.wait()
        red_send[i + 1] = red_send[i] + red_recv[i]

    sums = red_send[len(rounds)]
    norm = sums[:, 0:1] * (1.0 / total_pix)
    total = sums[:, LANES - 1 : LANES]
    row = lax.broadcasted_iota(jnp.int32, (padded, 1), 0)
    norm = jnp.where(row < bins, norm, 1.0)
    coefficient = (total / (total_pix * norm))[:bins]
    acc[0] = jnp.zeros((padded, chunk), F32)

    pl.when(has_right)(lambda: to_right.wait_send())
    pl.when(has_left)(lambda: to_left.wait_send())
    pl.when(has_above)(lambda: to_above.wait_send())
    pl.when(has_below)(lambda: to_below.wait_send())
    pl.when(has_left)(lambda: to_right.wait_recv())
    pl.when(has_right)(lambda: to_left.wait_recv())
    pl.when(has_below)(lambda: to_above.wait_recv())
    pl.when(has_above)(lambda: to_below.wait_recv())


    lax.fori_loop(0, min(border, blocks), stencil_step, 0)
    lax.fori_loop(max(blocks - border, border), blocks, stencil_step, 0)

    def c_copy(k):
        block = core * chunks + k
        return copy_to(mate, ratio.at[block], ratio.at[block], c_sems.at[0, k], c_sems.at[1, k])

    def unpacked(ref):
        full = bins // 8
        return jnp.concatenate(
            [
                jnp.concatenate(
                    [ref[i * full + r] for r in range(full)]
                    + [ref[2 * full][i * (bins % 8) : (i + 1) * (bins % 8)]],
                    axis=0,
                )
                for i in range(2)
            ],
            axis=1,
        )

    def back(j):
        cols = columns(j)
        kind = jnp.broadcast_to(classes_of[:, cols], (padded, chunk))
        value = ratio[j]
        high = value.astype(BF16).astype(F32)
        low = value - high
        spread = jnp.concatenate(
            [jnp.where(kind == c, x, 0.0).astype(BF16) for x in (high, low)
             for c in range(classes)],
            axis=0,
        ) if padded % 16 == 0 else jnp.concatenate(
            [jnp.where(kind == c, x, 0.0) for x in (high, low) for c in range(classes)], axis=0
        ).astype(BF16)
        both = jnp.dot(w_back[...], spread, preferred_element_type=F32)
        out[:, cols] += dens[:, cols] * (both[:shells] + both[shells:])
        out[0:1, cols] += RADIAL * low_recv[:, cols]
        out[shells - 1 : shells, cols] += RADIAL * high_recv[:, cols]

    def ratio_step(k, carry):
        for d in range(chips - 1):
            b_copy(k, d).wait_recv()
        block = core * chunks + k
        cols = columns(block)
        proj = unpacked(group_send.at[k])
        for d in range(chips - 1):
            proj = proj + unpacked(group_recv.at[d, k])
        number = counts[:, cols].astype(F32)
        masked = mask[:, cols]
        ratio[block, 0:bins] = number / proj - coefficient * masked
        ratio[block, bins:padded] = jnp.zeros((padded - bins, chunk), F32)
        acc[0, 0:bins] += number * jnp.log(masked * proj)
        c_copy(k).start()
        return carry

    def partner_step(k):
        c_copy(k).wait_recv()
        back(other * chunks + k)

    ratio_step(0, 0)
    back(core * chunks)

    def loop_step(k, carry):
        ratio_step(k, 0)
        back(core * chunks + k)
        partner_step(k - 1)
        return carry

    lax.fori_loop(1, chunks - 1, loop_step, 0)
    ratio_step(chunks - 1, 0)
    own_log = jnp.sum(jnp.sum(acc[0], axis=1, keepdims=True), axis=0, keepdims=True)
    scale = 1.0 / chips if chips > 2 else 1.0
    log_send[0] = jnp.broadcast_to(own_log * scale, (8, LANES))

    def log_copy(i):
        return copy_to(
            log_rounds[i], log_send.at[i], log_recv.at[i], log_sems.at[0, i], log_sems.at[1, i]
        )

    log_copy(0).start()
    back(core * chunks + chunks - 1)
    partner_step(chunks - 2)
    for i in range(len(log_rounds)):
        if i:
            log_copy(i).start()
        log_copy(i).wait()
        log_send[i + 1] = log_send[i] + log_recv[i]
    last = len(log_rounds)
    shares[0] = log_send[last]

    def share_copy(d):
        return copy_to(
            across[d - 1], log_send.at[last], shares.at[d], share_sems.at[0, d], share_sems.at[1, d]
        )

    for d in range(1, pix_count):
        share_copy(d).start()
    partner_step(chunks - 1)
    for d in range(1, pix_count):
        share_copy(d).wait()
    log_sum = shares[p]
    for q in range(1, pix_count):
        log_sum = log_sum + shares[(p + pix_count - q) % pix_count]

    safe_mean = jnp.where(row < bins, mean[...], 1.0)
    per_bin = jnp.where(
        row < bins, total * jnp.log(safe_mean / norm) - safe_mean * total_pix, 0.0
    )
    rest = jnp.sum(jnp.broadcast_to(per_bin, (padded, LANES)), axis=0, keepdims=True)
    loglik[...] = (log_sum + rest) * (1.0 / (bins * total_pix))

    def drain(k, carry):
        a_copy(k).wait_send()
        for d in range(chips - 1):
            b_copy(k, d).wait_send()
        c_copy(k).wait_send()
        return carry

    lax.fori_loop(0, chunks, drain, 0)


def shards(pix_count, shell_count, field, momentum, kernels, depth_class, counts, mask, mean_counts, shell_scale):
    shells, pixels = field.shape
    classes, bins, _ = kernels.shape
    padded = -(-bins // 8) * 8
    assert bins % 8 == 4
    chunk = 1024
    while pixels % (2 * chunk):
        chunk //= 2
    chunks = pixels // (2 * chunk)
    chips = shell_count // 2
    weight = jnp.pad(kernels, ((0, 0), (0, padded - bins), (0, 0))).reshape(classes * padded, shells)
    mean = jnp.pad(mean_counts, (0, padded - bins), constant_values=1.0)[:, None]
    diag = (1.0 / (shell_scale * shell_scale) + 4.0 * ANGULAR + 2.0 * RADIAL)[:, None]
    steps = (pix_count.bit_length() - 1) + (shell_count.bit_length() - 1)
    tiles = 2 * (bins // 8) + 1
    vmem = pltpu.VMEM
    dma = pltpu.SemaphoreType.DMA
    edge = vmem((1, pixels), F32)
    part = vmem((chunks, padded, chunk), F32)
    scratch = [
        vmem((shells, pixels + 2 * CYCLE), F32),
        vmem((shells, pixels), F32),
        part, part, part,
        vmem((chunks, tiles, 8, chunk // 2), F32),
        vmem((chips - 1, chunks, tiles, 8, chunk // 2), F32),
        vmem((2 * chunks, padded, chunk), F32),
        edge, edge, edge, edge,
        vmem((2, padded, chunk), F32),
        vmem((steps + 1, padded, LANES), F32),
        vmem((steps, padded, LANES), F32),
        vmem((steps + 1, 8, LANES), F32),
        vmem((steps, 8, LANES), F32),
        vmem((pix_count, 8, LANES), F32),
        vmem((classes * padded, 3 * shells), BF16),
        vmem((2 * shells, 2 * classes * padded), BF16),
        dma((2, chunks)),
        dma((chips - 1, chunks)),
        dma((chips - 1, chunks)),
        dma((2, chunks)),
        dma((4,)),
        dma((4,)),
        dma((2, steps)),
        dma((2, steps)),
        dma((2, pix_count)),
    ]
    gradient, loglik = pl.pallas_call(
        functools.partial(kernel, (pix_count, shell_count, classes, bins, chunk, chunks)),
        out_shape=(
            jax.ShapeDtypeStruct((shells, pixels), F32),
            jax.ShapeDtypeStruct((8, LANES), F32),
        ),
        in_specs=[pl.BlockSpec(memory_space=pltpu.VMEM)] * 9,
        out_specs=(pl.BlockSpec(memory_space=pltpu.VMEM), pl.BlockSpec(memory_space=pltpu.VMEM)),
        scratch_shapes=scratch,
        compiler_params=pltpu.CompilerParams(
            collective_id=0, has_side_effects=True, vmem_limit_bytes=56 * 2**20
        ),
    )(
        field, momentum, weight, weight.T, depth_class[None, :], counts, mask[None, :], mean, diag
    )
    return gradient, loglik[0, 0]


def solution(mesh):
    placed = (
        P("shell", "pix"),
        P("shell", "pix"),
        P(None, None, "shell"),
        P("pix"),
        P(None, "pix"),
        P("pix"),
        P(),
        P("shell"),
    )
    return jax.shard_map(
        functools.partial(shards, mesh.shape["pix"], mesh.shape["shell"]),
        mesh=mesh,
        in_specs=placed,
        out_specs=(P("shell", "pix"), P()),
        check_vma=False,
    )
```

```python
import functools

import jax
import jax.numpy as jnp
from jax import lax
from jax.experimental import pallas as pl
from jax.experimental.pallas import tpu as pltpu
from jax.sharding import PartitionSpec as P

CYCLE = 2048

LEAP = 0.1
ANGULAR = 0.5
RADIAL = 0.5
MESH = pl.DeviceIdType.MESH
F32 = jnp.float32
BF16 = jnp.bfloat16
LANES = 128


def halves(value):
    high = value.astype(BF16)
    return high, (value - high.astype(F32)).astype(BF16)


def kernel(
    sizes,
    field, momentum, weight, weight_t, classes_of, counts, mask, mean, diag,
    out, loglik,
    pos, dens, part_send, part_own, part_recv, group_send, group_recv, ratio,
    low_send, high_send, low_recv, high_recv, acc, red_send, red_recv, log_send, log_recv, shares,
    w_front, w_back,
    a_sems, b_send_sems, b_recv_sems, c_sems, halo_sems, edge_sems, red_sems, log_sems, share_sems,
):
    pix_count, shell_count, classes, bins, chunk, chunks = sizes
    chips = shell_count // 2
    shells, pixels = field.shape
    padded = weight.shape[0] // classes
    half = chunk // 2
    total_pix = pixels * pix_count
    p, s = lax.axis_index("pix"), lax.axis_index("shell")
    core, chip = s % 2, s // 2

    def flip(index, step):
        return index + step - 2 * step * ((index // step) % 2)

    mate = (p, flip(s, 1))
    peers = [(p, ((chip + d) % chips) * 2 + core) for d in range(1, chips)]
    rounds = []
    step = 1
    while step < shell_count:
        rounds.append((p, flip(s, step)))
        step *= 2
    step = 1
    while step < pix_count:
        rounds.append((flip(p, step), s))
        step *= 2
    log_rounds = [mate]
    if chips > 2:
        log_rounds += rounds[1 : shell_count.bit_length() - 1]
    across = [((p + d) % pix_count, s) for d in range(1, pix_count)]
    right, left = (p + 1) % pix_count, (p + pix_count - 1) % pix_count
    above, below = (s + 1) % shell_count, (s + shell_count - 1) % shell_count
    greeted = rounds[: shell_count.bit_length() - 1] + peers + across + [(p, above), (p, below)]
    barrier = pltpu.get_barrier_semaphore()
    for device in greeted:
        pl.semaphore_signal(barrier, inc=1, device_id=device, device_id_type=MESH)

    w_high, w_low = halves(weight[...])
    w_front[...] = jnp.concatenate([w_high, w_high, w_low], axis=1)
    t_high, t_low = halves(weight_t[...])
    w_back[...] = jnp.concatenate(
        [
            jnp.concatenate([t_high, t_high], axis=1),
            jnp.concatenate([t_low, jnp.zeros_like(t_low)], axis=1),
        ],
        axis=0,
    )
    acc[...] = jnp.zeros_like(acc)

    def copy_to(device, src, dst, send_sem, recv_sem):
        return pltpu.make_async_remote_copy(
            src_ref=src, dst_ref=dst, send_sem=send_sem, recv_sem=recv_sem,
            device_id=device, device_id_type=MESH,
        )

    def columns(j, lead=0):
        return pl.ds(pl.multiple_of(j * chunk + lead, LANES), chunk)

    def front(j, target):
        cols = columns(j)
        here = field[:, cols] + LEAP * momentum[:, cols]
        pos[:, columns(j, CYCLE)] = here
        density = jnp.exp(here)
        dens[:, cols] = density
        high, low = halves(density)
        every = jnp.dot(
            w_front[...], jnp.concatenate([high, low, high], axis=0), preferred_element_type=F32
        )
        kind = jnp.broadcast_to(classes_of[:, cols], (padded, chunk))
        part = every[:padded]
        for c in range(1, classes):
            part = jnp.where(kind == c, every[c * padded : (c + 1) * padded], part)
        target[...] = part
        acc[0] += mask[:, cols] * part
        acc[1, 0:bins] += counts[:, cols].astype(F32)

    def a_copy(k):
        return copy_to(mate, part_send.at[k], part_recv.at[k], a_sems.at[0, k], a_sems.at[1, k])

    def b_copy(k, d):
        return copy_to(
            peers[d], group_send.at[k], group_recv.at[d, k], b_send_sems.at[d, k], b_recv_sems.at[d, k]
        )

    def forward(k):
        a_copy(k).wait_recv()
        both = part_own[k] + part_recv[k]
        full = bins // 8
        for i in range(2):
            for r in range(full):
                group_send[k, i * full + r] = both[r * 8 : r * 8 + 8, i * half : (i + 1) * half]
        group_send[k, 2 * full] = jnp.concatenate(
            [both[full * 8 : bins, :half], both[full * 8 : bins, half:]], axis=0
        )
        for d in range(chips - 1):
            b_copy(k, d).start()

    other = 1 - core
    low_send[...] = field[0:1, :] + LEAP * momentum[0:1, :]
    high_send[...] = field[shells - 1 : shells, :] + LEAP * momentum[shells - 1 : shells, :]
    to_above = copy_to((p, above), high_send, low_recv, edge_sems.at[0], edge_sems.at[1])
    to_below = copy_to((p, below), low_send, high_recv, edge_sems.at[2], edge_sems.at[3])
    has_above, has_below = s < shell_count - 1, s > 0
    front(other * chunks, part_send.at[0])
    pl.semaphore_wait(barrier, len(greeted))
    pl.when(has_above)(lambda: to_above.start())
    pl.when(has_below)(lambda: to_below.start())
    a_copy(0).start()
    front(core * chunks, part_own.at[0])

    def front_step(k, carry):
        front(other * chunks + k, part_send.at[k])
        front(core * chunks + k, part_own.at[k])
        a_copy(k).start()
        forward(k - 1)
        return carry

    lax.fori_loop(1, chunks, front_step, 0)
    forward(chunks - 1)

    to_right = copy_to(
        (right, s), pos.at[:, pl.ds(pixels, CYCLE)], pos.at[:, pl.ds(0, CYCLE)],
        halo_sems.at[0], halo_sems.at[1],
    )
    to_left = copy_to(
        (left, s), pos.at[:, pl.ds(CYCLE, CYCLE)], pos.at[:, pl.ds(pixels + CYCLE, CYCLE)],
        halo_sems.at[2], halo_sems.at[3],
    )
    has_right, has_left = p < pix_count - 1, p > 0
    pl.when(has_right)(lambda: to_right.start())
    pl.when(has_left)(lambda: to_left.start())

    @pl.when(p == 0)
    def _():
        pos[:, 0:CYCLE] = jnp.zeros((shells, CYCLE), F32)

    @pl.when(p == pix_count - 1)
    def _():
        pos[:, pixels + CYCLE :] = jnp.zeros((shells, CYCLE), F32)

    @pl.when(s == 0)
    def _():
        low_recv[...] = jnp.zeros_like(low_recv)

    @pl.when(s == shell_count - 1)
    def _():
        high_recv[...] = jnp.zeros_like(high_recv)

    lane = lax.broadcasted_iota(jnp.int32, (padded, LANES), 1)
    weighted = jnp.sum(acc[0], axis=1, keepdims=True)
    counted = jnp.sum(acc[1], axis=1, keepdims=True) * (1.0 / shell_count)
    red_send[0] = jnp.where(lane < LANES // 2, weighted, counted)

    scaled = diag[...]

    def stencil_step(j, carry):
        cols = columns(j)
        wide = pos[:, pl.ds(pl.multiple_of(j * chunk + CYCLE - LANES, LANES), chunk + 2 * LANES)]
        here = wide[:, LANES : LANES + chunk]
        around = (
            wide[:, LANES - 1 : LANES - 1 + chunk]
            + wide[:, LANES + 1 : LANES + 1 + chunk]
            + pos[:, columns(j)]
            + pos[:, columns(j, 2 * CYCLE)]
        )
        lower = jnp.concatenate([jnp.zeros((1, chunk), F32), here[:-1]], axis=0)
        upper = jnp.concatenate([here[1:], jnp.zeros((1, chunk), F32)], axis=0)
        out[:, cols] = ANGULAR * around + RADIAL * (lower + upper) - here * scaled
        return carry

    across_chips = rounds[1 : shell_count.bit_length() - 1]
    order = rounds[:1] + rounds[shell_count.bit_length() - 1 :] + across_chips
    early = len(order) - 1

    def red_copy(i):
        return copy_to(
            order[i], red_send.at[i], red_recv.at[i], red_sems.at[0, i], red_sems.at[1, i]
        )

    blocks, border = pixels // chunk, -(-CYCLE // chunk)
    inner = max(blocks - 2 * border, 0)
    for i in range(early):
        red_copy(i).start()
        lax.fori_loop(
            border + inner * i // early, border + inner * (i + 1) // early, stencil_step, 0
        )
        red_copy(i).wait()
        red_send[i + 1] = red_send[i] + red_recv[i]
    red_copy(early).start()

    acc[0] = jnp.zeros((padded, chunk), F32)

    pl.when(has_right)(lambda: to_right.wait_send())
    pl.when(has_left)(lambda: to_left.wait_send())
    pl.when(has_above)(lambda: to_above.wait_send())
    pl.when(has_below)(lambda: to_below.wait_send())
    pl.when(has_left)(lambda: to_right.wait_recv())
    pl.when(has_right)(lambda: to_left.wait_recv())
    pl.when(has_below)(lambda: to_above.wait_recv())
    pl.when(has_above)(lambda: to_below.wait_recv())


    lax.fori_loop(0, min(border, blocks), stencil_step, 0)
    lax.fori_loop(max(blocks - border, border), blocks, stencil_step, 0)

    def c_copy(k):
        block = core * chunks + k
        return copy_to(mate, ratio.at[block], ratio.at[block], c_sems.at[0, k], c_sems.at[1, k])

    def unpacked(ref):
        full = bins // 8
        return jnp.concatenate(
            [
                jnp.concatenate(
                    [ref[i * full + r] for r in range(full)]
                    + [ref[2 * full][i * (bins % 8) : (i + 1) * (bins % 8)]],
                    axis=0,
                )
                for i in range(2)
            ],
            axis=1,
        )

    def ratio_step(k, carry):
        for d in range(chips - 1):
            b_copy(k, d).wait_recv()
        block = core * chunks + k
        cols = columns(block)
        proj = unpacked(group_send.at[k])
        for d in range(chips - 1):
            proj = proj + unpacked(group_recv.at[d, k])
        number = counts[:, cols].astype(F32)
        masked = mask[:, cols]
        ratio[block, 0:bins] = number / proj
        ratio[block, bins:padded] = jnp.zeros((padded - bins, chunk), F32)
        acc[0, 0:bins] += number * jnp.log(masked * proj)
        c_copy(k).start()
        return carry

    lax.fori_loop(0, chunks, ratio_step, 0)
    own_log = jnp.sum(jnp.sum(acc[0], axis=1, keepdims=True), axis=0, keepdims=True)
    scale = 1.0 / chips if chips > 2 else 1.0
    log_send[0] = jnp.broadcast_to(own_log * scale, (8, LANES))

    def log_copy(i):
        return copy_to(
            log_rounds[i], log_send.at[i], log_recv.at[i], log_sems.at[0, i], log_sems.at[1, i]
        )

    log_copy(0).start()
    red_copy(early).wait()
    sums = red_send[early] + red_recv[early]
    norm = sums[:, 0:1] * (1.0 / total_pix)
    total = sums[:, LANES - 1 : LANES]
    row = lax.broadcasted_iota(jnp.int32, (padded, 1), 0)
    norm = jnp.where(row < bins, norm, 1.0)
    coefficient = total / (total_pix * norm)

    def back(j):
        cols = columns(j)
        kind = jnp.broadcast_to(classes_of[:, cols], (padded, chunk))
        value = ratio[j] - coefficient * mask[:, cols]
        high = value.astype(BF16).astype(F32)
        low = value - high
        spread = jnp.concatenate(
            [jnp.where(kind == c, x, 0.0).astype(BF16) for x in (high, low)
             for c in range(classes)],
            axis=0,
        ) if padded % 16 == 0 else jnp.concatenate(
            [jnp.where(kind == c, x, 0.0) for x in (high, low) for c in range(classes)], axis=0
        ).astype(BF16)
        both = jnp.dot(w_back[...], spread, preferred_element_type=F32)
        out[:, cols] += dens[:, cols] * (both[:shells] + both[shells:])
        out[0:1, cols] += RADIAL * low_recv[:, cols]
        out[shells - 1 : shells, cols] += RADIAL * high_recv[:, cols]

    def own_step(k, carry):
        back(core * chunks + k)
        return carry

    def partner_step(k, carry):
        c_copy(k).wait_recv()
        back(other * chunks + k)
        return carry

    lax.fori_loop(0, chunks, own_step, 0)
    for i in range(len(log_rounds)):
        if i:
            log_copy(i).start()
        log_copy(i).wait()
        log_send[i + 1] = log_send[i] + log_recv[i]
    last = len(log_rounds)
    shares[0] = log_send[last]

    def share_copy(d):
        return copy_to(
            across[d - 1], log_send.at[last], shares.at[d], share_sems.at[0, d], share_sems.at[1, d]
        )

    for d in range(1, pix_count):
        share_copy(d).start()
    lax.fori_loop(0, chunks, partner_step, 0)
    for d in range(1, pix_count):
        share_copy(d).wait()
    log_sum = shares[p]
    for q in range(1, pix_count):
        log_sum = log_sum + shares[(p + pix_count - q) % pix_count]

    safe_mean = jnp.where(row < bins, mean[...], 1.0)
    per_bin = jnp.where(
        row < bins, total * jnp.log(safe_mean / norm) - safe_mean * total_pix, 0.0
    )
    rest = jnp.sum(jnp.broadcast_to(per_bin, (padded, LANES)), axis=0, keepdims=True)
    loglik[...] = (log_sum + rest) * (1.0 / (bins * total_pix))

    def drain(k, carry):
        a_copy(k).wait_send()
        for d in range(chips - 1):
            b_copy(k, d).wait_send()
        c_copy(k).wait_send()
        return carry

    lax.fori_loop(0, chunks, drain, 0)


def shards(pix_count, shell_count, field, momentum, kernels, depth_class, counts, mask, mean_counts, shell_scale):
    shells, pixels = field.shape
    classes, bins, _ = kernels.shape
    padded = -(-bins // 8) * 8
    assert bins % 8 == 4
    chunk = 1024
    while pixels % (2 * chunk):
        chunk //= 2
    chunks = pixels // (2 * chunk)
    chips = shell_count // 2
    weight = jnp.pad(kernels, ((0, 0), (0, padded - bins), (0, 0))).reshape(classes * padded, shells)
    mean = jnp.pad(mean_counts, (0, padded - bins), constant_values=1.0)[:, None]
    diag = (1.0 / (shell_scale * shell_scale) + 4.0 * ANGULAR + 2.0 * RADIAL)[:, None]
    steps = (pix_count.bit_length() - 1) + (shell_count.bit_length() - 1)
    tiles = 2 * (bins // 8) + 1
    vmem = pltpu.VMEM
    dma = pltpu.SemaphoreType.DMA
    edge = vmem((1, pixels), F32)
    part = vmem((chunks, padded, chunk), F32)
    scratch = [
        vmem((shells, pixels + 2 * CYCLE), F32),
        vmem((shells, pixels), F32),
        part, part, part,
        vmem((chunks, tiles, 8, chunk // 2), F32),
        vmem((chips - 1, chunks, tiles, 8, chunk // 2), F32),
        vmem((2 * chunks, padded, chunk), F32),
        edge, edge, edge, edge,
        vmem((2, padded, chunk), F32),
        vmem((steps + 1, padded, LANES), F32),
        vmem((steps, padded, LANES), F32),
        vmem((steps + 1, 8, LANES), F32),
        vmem((steps, 8, LANES), F32),
        vmem((pix_count, 8, LANES), F32),
        vmem((classes * padded, 3 * shells), BF16),
        vmem((2 * shells, 2 * classes * padded), BF16),
        dma((2, chunks)),
        dma((chips - 1, chunks)),
        dma((chips - 1, chunks)),
        dma((2, chunks)),
        dma((4,)),
        dma((4,)),
        dma((2, steps)),
        dma((2, steps)),
        dma((2, pix_count)),
    ]
    gradient, loglik = pl.pallas_call(
        functools.partial(kernel, (pix_count, shell_count, classes, bins, chunk, chunks)),
        out_shape=(
            jax.ShapeDtypeStruct((shells, pixels), F32),
            jax.ShapeDtypeStruct((8, LANES), F32),
        ),
        in_specs=[pl.BlockSpec(memory_space=pltpu.VMEM)] * 9,
        out_specs=(pl.BlockSpec(memory_space=pltpu.VMEM), pl.BlockSpec(memory_space=pltpu.VMEM)),
        scratch_shapes=scratch,
        compiler_params=pltpu.CompilerParams(
            collective_id=0, has_side_effects=True, vmem_limit_bytes=56 * 2**20
        ),
    )(
        field, momentum, weight, weight.T, depth_class[None, :], counts, mask[None, :], mean, diag
    )
    return gradient, loglik[0, 0]


def solution(mesh):
    placed = (
        P("shell", "pix"),
        P("shell", "pix"),
        P(None, None, "shell"),
        P("pix"),
        P(None, "pix"),
        P("pix"),
        P(),
        P("shell"),
    )
    return jax.shard_map(
        functools.partial(shards, mesh.shape["pix"], mesh.shape["shell"]),
        mesh=mesh,
        in_specs=placed,
        out_specs=(P("shell", "pix"), P()),
        check_vma=False,
    )
```
